32 devices in a mesh: dp: 8 (over z, y), expert: 4 (over x, core).
Axes of the slice: x: 2, y: 2, z: 4, core: 2. Of those that a mesh axis runs over, the one named last changes fastest.
Arguments:
- tokens: bfloat16 [4096, 3584], P(('dp', 'expert')), may hold values from -6 to 6
- routes: int32 [4096, 1], P(('dp', 'expert')), may hold values from 0 to 3; in each aligned block of 128 rows (0 to 127, 128 to 255, ...) at most 48 rows name the same one
- gates: float32 [4096, 1], P(('dp', 'expert')), may hold values from 0.1 to 1
- counts: int32 [32], P(('dp', 'expert')), may hold values from 16 to 128, as said below
- expert_weight: bfloat16 [4, 3584, 1024], P('expert'), may hold values from -0.09375 to 0.09375
- cotangent: bfloat16 [4096, 1024], P(('dp', 'expert')), may hold values from -6 to 6
Outputs:
- mixed: bfloat16 [4096, 1024], P(('dp', 'expert'))
- token_grad: bfloat16 [4096, 3584], P(('dp', 'expert'))
- gate_grad: float32 [4096, 1], P(('dp', 'expert'))
The draws below stay inside these ranges and needn't reach their ends.
Inputs may be any that keep to these rules, and one draw needn't show every extreme that they name: `routes`: among the tokens of one device at most 48 name one expert; some device sends exactly 48 to some expert; every expert is named. The first counts[i] tokens of device i are valid; some device has all of its tokens valid.
All inputs are finite; a program needn't handle non-finite values.
Results may differ from the reference program's by a relative error of at most 0.0058.
Values may be sent and summed in bfloat16 or wider, within the bound.
A program may use at most 64 MiB of HBM per device.

```python
import math
import jax
import jax.numpy as jnp
import numpy as np
from jax import lax

D = 3584
H = 1024
TOK_DEV = 128
EXPERTS = 4
CAP = 48
TOKENS = 4096
N_EXPERT = 4
DEVICES = 32


def draw_counts(key, part):
    number = DEVICES
    level = jax.random.randint(jax.random.fold_in(key, 11), (), TOK_DEV // 8, TOK_DEV // 4 + 1)
    upward = jax.random.randint(jax.random.fold_in(key, 12), (), 0, 2)
    index = jnp.arange(number, dtype=jnp.int32)
    place = jnp.where(upward == 1, index, number - 1 - index).astype(jnp.int32)
    ramp = level + 2 * level * place // max(number - 1, 1)
    noise = jax.random.randint(jax.random.fold_in(key, 13), (number,), 0, 1048576)
    jitter = noise % (ramp + 1)
    values = jnp.minimum(TOK_DEV, ramp + jitter)
    full_one = jax.random.randint(jax.random.fold_in(key, 14), (), 0, number)
    offset = jax.random.randint(jax.random.fold_in(key, 15), (), 0, number - 1)
    low_one = (full_one + 1 + offset) % number
    values = jnp.where(index == full_one, TOK_DEV, values)
    values = jnp.where(index == low_one, TOK_DEV // 8, values)
    return values.astype(jnp.int32)


def levels(key, shape, pieces, least, top_value):
    def one(dim, blocks):
        heights = jax.random.uniform(jax.random.fold_in(jax.random.fold_in(key, 6), dim), (blocks,), jnp.float32, least / len(pieces), top_value / len(pieces))
        return jnp.repeat(jnp.exp(heights), shape[dim] // blocks).reshape((-1,) + (1,) * (len(shape) - dim - 1))

    level = one(*pieces[0])
    for cut in pieces[1:]:
        level = level * one(*cut)
    return level


def shared_out(rng, own, number, rows, amount, top, most, lean):
    order = jax.random.permutation(rng, amount)
    heavy_load, common = shares(amount, rows * top, most, lean, True), shares(amount, rows * top, most, lean, False)
    places = jnp.arange(amount)

    def named(lengths, offset_by):
        used = int((lengths > 0).sum())
        fixed = max(1, used // 4)
        moved = fixed + (places - fixed + offset_by * (used - fixed)) % max(1, amount - fixed)
        return jnp.zeros((amount,), jnp.int32).at[order[jnp.where(places < fixed, places, moved)]].set(jnp.asarray(lengths, jnp.int32))

    lengths = jnp.where(number % 4 == 0, named(heavy_load, number // 4), named(common, number - number // 4 - 1))
    mixed = jax.random.permutation(jax.random.fold_in(own, 3), amount)
    source_of, sink = mixed[0:amount // 2 * 2:2], mixed[1:amount // 2 * 2:2]
    margin = jnp.minimum(lengths[source_of] - 1, most - lengths[sink]) // 2
    margin = jnp.where((source_of == order[0]) | (sink == order[0]) | (lengths[sink] == 0), 0, jnp.maximum(margin, 0))
    moved = jax.random.randint(jax.random.fold_in(own, 4), (amount // 2,), 0, 1 << 20) % (margin + 1)
    lengths = lengths.at[source_of].add(-moved).at[sink].add(moved)
    labels = jnp.searchsorted(jnp.cumsum(lengths), jnp.arange(rows * top), side="right").astype(jnp.int32)
    grid = labels.reshape(top, rows).T
    grid = grid[jax.random.permutation(jax.random.fold_in(own, 1), rows)]
    offset_by = jax.random.randint(jax.random.fold_in(own, 2), (rows, 1), 0, top)
    return jnp.take_along_axis(grid, (jnp.arange(top)[None, :] + offset_by) % top, axis=1)


def shares(amount, total, reach, skew, full):
    weights = [(1 << 20) // math.isqrt(rank ** skew) + 1 for rank in range(1, amount + 1)]
    largest = reach if full else min(reach, max(-(-total // amount), total * weights[0] // sum(weights)))
    least = 1 if total - largest >= amount - 1 else 0
    given, rest = [largest] + [least] * (amount - 1), total - largest - least * (amount - 1)
    while rest > 0:
        free = [i for i in range(1, amount) if given[i] < largest] or [i for i in range(1, amount) if given[i] < reach]
        pool, budget = sum([weights[i] for i in free]), rest
        for i in free:
            more = min(reach - given[i], max(1, budget * weights[i] // pool), rest)
            given[i] = given[i] + more
            rest = rest - more
    return np.array(given)


def centred(stream_key, extent, width, bound, pieces=(), kind=jnp.bfloat16):
    result = jax.random.normal(stream_key, extent, jnp.float32) * width
    if len(pieces) > 0:
        result = levels(stream_key, extent, pieces, -0.22, 0.18) * result
    return jnp.clip(result, min=-bound, max=bound).astype(kind)


def setup_inputs(seed: int = 0) -> dict:
    arg_keys = jax.random.split(jax.random.key(seed), 7)
    tokens = centred(arg_keys[0], (TOKENS, D), 1.0, 6.0, ((0, 32),))
    routes_keys = jax.random.split(jax.random.fold_in(arg_keys[1], 1), TOKENS // TOK_DEV)
    routes_turns = jax.random.permutation(jax.random.fold_in(arg_keys[1], 3), TOKENS // TOK_DEV)
    routes = jax.vmap(lambda own, number: shared_out(jax.random.fold_in(arg_keys[1], 2), own, number, TOK_DEV, N_EXPERT, 1, CAP, 2))(routes_keys, routes_turns).reshape((TOKENS, 1))
    gates = jnp.clip(jnp.exp(math.log(1.0) - 2.3025851 * jax.random.uniform(arg_keys[2], (TOKENS, 1), jnp.float32) ** levels(arg_keys[2], (TOKENS, 1), ((0, 32),), -0.2, 0.2)), 0.1, 1.0)
    counts = draw_counts(jax.random.fold_in(arg_keys[6], 71), 0)
    expert_weight = centred(arg_keys[4], (EXPERTS, D, H), D ** -0.5, 0.09375, ((0, 4),))
    cotangent = centred(arg_keys[5], (TOKENS, H), 1.0, 6.0, ((0, 32),))
    return dict(tokens=tokens, routes=routes, gates=gates, counts=counts, expert_weight=expert_weight, cotangent=cotangent)


def reference(tokens, routes, gates, counts, expert_weight, cotangent):
    total_rows = tokens.shape[0]
    route = routes[:, 0]
    gate = gates[:, 0]
    position = jnp.arange(total_rows, dtype=jnp.int32)
    owner = (position // TOK_DEV).astype(jnp.int32)
    valid = ((position % TOK_DEV) < counts[owner]).astype(jnp.float32)
    total = jnp.sum(counts.astype(jnp.float32))
    scale = jnp.float32(total_rows) / total
    factor = valid * scale
    upstream = ((gate * factor)[:, None] * cotangent.astype(jnp.float32)).astype(jnp.bfloat16)
    order = jnp.argsort(route, stable=True).astype(jnp.int32)
    loads = jnp.bincount(route, length=EXPERTS).astype(jnp.int32)
    starts = (jnp.cumsum(loads) - loads).astype(jnp.int32)
    span = DEVICES * CAP
    padded_order = jnp.concatenate([order, jnp.zeros((span,), jnp.int32)])

    def step(carry, expert):
        act_all, grad_all = carry
        index = lax.dynamic_slice_in_dim(padded_order, starts[expert], span)
        live = jnp.arange(span, dtype=jnp.int32) < loads[expert]
        target = jnp.where(live, index, total_rows).astype(jnp.int32)
        weight = expert_weight[expert]
        pre = jnp.dot(tokens[index], weight, preferred_element_type=jnp.float32)
        sig = jax.nn.sigmoid(pre)
        act = (pre * sig).astype(jnp.bfloat16)
        slope = sig * (1.0 + pre * (1.0 - sig))
        delta = (upstream[index].astype(jnp.float32) * slope).astype(jnp.bfloat16)
        back = jnp.dot(delta, weight.T, preferred_element_type=jnp.float32).astype(jnp.bfloat16)
        act_all = act_all.at[target].set(act, mode="drop")
        grad_all = grad_all.at[target].set(back, mode="drop")
        return (act_all, grad_all), None

    start = (jnp.zeros((total_rows, H), jnp.bfloat16), jnp.zeros((total_rows, D), jnp.bfloat16))
    (act_all, grad_all), _ = lax.scan(step, start, jnp.arange(EXPERTS, dtype=jnp.int32))
    act_float = act_all.astype(jnp.float32)
    mixed = (gate[:, None] * act_float).astype(jnp.bfloat16)
    gate_grad = (jnp.sum(act_float * cotangent.astype(jnp.float32), axis=1) * factor)[:, None]
    return mixed, grad_all, gate_grad
```

```python
import functools

import jax
import jax.numpy as jnp
from jax import lax
from jax.experimental import pallas as pl
from jax.experimental.pallas import tpu as pltpu
from jax.sharding import PartitionSpec as P

MESH = pl.DeviceIdType.MESH
ROWS = 16
TOK, COT, ACT, GRAD = 0, 1, 2, 3


def tile_of(size, most):
    tile = most
    while size % tile:
        tile //= 2
    return tile


def kernel(
    n, groups, cap, routes_ref, gates_ref, counts_ref, tokens_hbm, weight_hbm, cotangent_hbm,
    mixed_hbm, grad_hbm, gate_grad_ref,
    tok, cot, w, place, unplace, tok_out, cot_out, tok_in, cot_in, delta,
    act_out, grad_out, act_home, grad_home, mixed_v, grad_v, cnt_mine, cnt_dp, cnt_sum, cnt_ex,
    load_sem, store_sem, send_sem, recv_sem, cnt_send, cnt_recv,
):
    rows, depth = tok.shape
    units = cot.shape[1]
    slots = n * cap
    pieces = cap // ROWS
    far = n - 2
    step = far * ROWS
    me = lax.axis_index("expert")
    group = lax.axis_index("dp")

    load_tok = pltpu.make_async_copy(tokens_hbm, tok, load_sem.at[0])
    load_cot = pltpu.make_async_copy(cotangent_hbm, cot, load_sem.at[1])
    load_w = pltpu.make_async_copy(weight_hbm.at[0], w, load_sem.at[2])
    load_tok.start()
    load_cot.start()
    load_w.start()

    barrier = pltpu.get_barrier_semaphore()
    for j in range(1, n):
        pl.semaphore_signal(
            barrier, inc=1, device_id=(group, lax.bitwise_xor(me, j)), device_id_type=MESH
        )
    for k in range(1, groups):
        pl.semaphore_signal(
            barrier, inc=1, device_id=(lax.rem(group + k, groups), me), device_id_type=MESH
        )

    route = routes_ref[...]
    high = -(-n // ROWS) * ROWS
    choose = lax.broadcasted_iota(jnp.int32, (high, rows), 0) == route
    choose_f = jnp.where(choose, 1.0, 0.0)
    upper = jnp.where(
        lax.broadcasted_iota(jnp.int32, (rows, rows), 0)
        <= lax.broadcasted_iota(jnp.int32, (rows, rows), 1),
        1.0,
        0.0,
    ).astype(jnp.bfloat16)
    running = jnp.dot(choose_f.astype(jnp.bfloat16), upper, preferred_element_type=jnp.float32)
    rank = (jnp.sum(running * choose_f, axis=0, keepdims=True) - 1.0).astype(jnp.int32)
    rel = lax.bitwise_xor(route, jnp.full(route.shape, me, jnp.int32))
    piece = lax.div(rank, jnp.int32(ROWS))
    slot = jnp.where(
        rel < 2,
        rel * cap + rank,
        2 * cap + piece * step + (rel - 2) * ROWS + (rank - piece * ROWS),
    )
    place[...] = jnp.where(
        lax.broadcasted_iota(jnp.int32, (slots, rows), 0) == slot, 1.0, 0.0
    ).astype(jnp.bfloat16)
    line = lax.broadcasted_iota(jnp.int32, (128, rows), 0)
    columns = jnp.transpose(
        jnp.where(line == 0, gates_ref[...], jnp.where(line == 1, slot.astype(jnp.float32), 0.0))
    )
    gate = columns[:, 0:1]
    unplace[...] = jnp.where(
        lax.broadcasted_iota(jnp.int32, (rows, slots), 1) == columns[:, 1:2].astype(jnp.int32),
        1.0,
        0.0,
    ).astype(jnp.bfloat16)
    count = counts_ref[0]
    cnt_mine[...] = jnp.full(cnt_mine.shape, count.astype(jnp.float32), jnp.float32)

    def remote(kind, source, target, j, part, at, size):
        return pltpu.make_async_remote_copy(
            src_ref=source.at[pl.ds(at, size)],
            dst_ref=target.at[pl.ds(at, size)],
            send_sem=send_sem.at[kind, j, part],
            recv_sem=recv_sem.at[kind, j, part],
            device_id=(group, lax.bitwise_xor(me, j)),
            device_id_type=MESH,
        )

    def gather(source, target, at, size):
        width = tile_of(source.shape[1], 512)

        def body(i, carry):
            cut = pl.ds(pl.multiple_of(i * width, width), width)
            target[at : at + size, cut] = jnp.dot(
                place[at : at + size, :], source[:, cut], preferred_element_type=jnp.float32
            ).astype(jnp.bfloat16)
            return carry

        lax.fori_loop(0, source.shape[1] // width, body, 0)

    def far_at(part, j):
        return 2 * cap + part * step + (j - 2) * ROWS

    out = []

    load_tok.wait()
    for part in range(pieces):
        gather(tok, tok_out, 2 * cap + part * step, step)
        if part == 0:
            load_cot.wait()
            pl.semaphore_wait(barrier, n - 1 + groups - 1)
        for j in range(2, n):
            copy = remote(TOK, tok_out, tok_in, j, part, far_at(part, j), ROWS)
            copy.start()
            out.append(copy)
        gather(cot, cot_out, 2 * cap + part * step, step)
        for j in range(2, n):
            copy = remote(COT, cot_out, cot_in, j, part, far_at(part, j), ROWS)
            copy.start()
            out.append(copy)
        if part == 0:
            gather(tok, tok_out, cap, cap)
            near_tok = remote(TOK, tok_out, tok_in, 1, 0, cap, cap)
            near_tok.start()
            gather(cot, cot_out, cap, cap)
            near_cot = remote(COT, cot_out, cot_in, 1, 0, cap, cap)
            near_cot.start()

    counts = []
    for k in range(1, groups):
        copy = pltpu.make_async_remote_copy(
            src_ref=cnt_mine,
            dst_ref=cnt_dp.at[k - 1],
            send_sem=cnt_send.at[k - 1],
            recv_sem=cnt_recv.at[k - 1],
            device_id=(lax.rem(group + k, groups), me),
            device_id_type=MESH,
        )
        copy.start()
        counts.append(copy)

    gather(tok, tok_in, 0, cap)
    gather(cot, cot_in, 0, cap)

    def forward(at, size, kept):
        width = tile_of(units, 256)

        def body(i, carry):
            cut = pl.ds(pl.multiple_of(i * width, width), width)
            pre = jnp.dot(
                tok_in[at : at + size, :], w[:, cut], preferred_element_type=jnp.float32
            )
            sig = jax.nn.sigmoid(pre)
            act = (pre * sig).astype(jnp.bfloat16)
            if kept:
                act_home[at : at + kept, cut] = act[:kept]
            act_out[at + kept : at + size, cut] = act[kept:]
            slope = sig * (1.0 + pre * (1.0 - sig))
            delta[0:size, cut] = (
                cot_in[at : at + size, cut].astype(jnp.float32) * slope
            ).astype(jnp.bfloat16)
            return carry

        lax.fori_loop(0, units // width, body, 0)

    def backward(at, size, kept):
        width = tile_of(depth, 512)

        def body(i, carry):
            cut = pl.ds(pl.multiple_of(i * width, width), width)
            grad = lax.dot_general(
                delta[0:size, :], w[cut, :], (((1,), (1,)), ((), ())),
                preferred_element_type=jnp.float32,
            ).astype(jnp.bfloat16)
            if kept:
                grad_home[at : at + kept, cut] = grad[:kept]
            grad_out[at + kept : at + size, cut] = grad[kept:]
            return carry

        lax.fori_loop(0, depth // width, body, 0)

    load_w.wait()
    near_tok.wait_recv()
    near_cot.wait_recv()
    forward(0, 2 * cap, cap)
    near_act = remote(ACT, act_out, act_home, 1, 0, cap, cap)
    near_act.start()
    backward(0, 2 * cap, cap)
    near_grad = remote(GRAD, grad_out, grad_home, 1, 0, cap, cap)
    near_grad.start()

    for copy in counts:
        copy.wait_recv()
    partial = cnt_mine[...]
    for k in range(1, groups):
        partial = partial + cnt_dp[k - 1]
    cnt_sum[...] = partial
    sums = []
    for j in range(1, n):
        copy = pltpu.make_async_remote_copy(
            src_ref=cnt_sum,
            dst_ref=cnt_ex.at[j - 1],
            send_sem=cnt_send.at[groups - 1 + j - 1],
            recv_sem=cnt_recv.at[groups - 1 + j - 1],
            device_id=(group, lax.bitwise_xor(me, j)),
            device_id_type=MESH,
        )
        copy.start()
        sums.append(copy)

    for part in range(pieces):
        at = 2 * cap + part * step
        for kind in (TOK, COT):
            for j in range(2, n):
                if kind == TOK:
                    remote(TOK, tok_out, tok_in, j, part, far_at(part, j), ROWS).wait_recv()
                else:
                    remote(COT, cot_out, cot_in, j, part, far_at(part, j), ROWS).wait_recv()
        forward(at, step, 0)
        for j in range(2, n):
            copy = remote(ACT, act_out, act_home, j, part, far_at(part, j), ROWS)
            copy.start()
        backward(at, step, 0)
        for j in range(2, n):
            copy = remote(GRAD, grad_out, grad_home, j, part, far_at(part, j), ROWS)
            copy.start()

    for copy in out:
        copy.wait_send()
    near_tok.wait_send()
    near_cot.wait_send()
    for copy in counts:
        copy.wait_send()
    for copy in sums:
        copy.wait()
    total = partial
    for j in range(1, n):
        total = total + cnt_ex[j - 1]
    scale = jnp.float32(rows * groups * n) / total[0:1, 0:1]
    position = lax.broadcasted_iota(jnp.int32, (rows, 1), 0)
    factor = jnp.where(position < count, 1.0, 0.0) * scale

    near_act.wait()
    for part in range(pieces):
        for j in range(2, n):
            remote(ACT, act_out, act_home, j, part, far_at(part, j), ROWS).wait()
    act = jnp.dot(unplace[...], act_home[...], preferred_element_type=jnp.float32)
    mixed_v[...] = (gate * act).astype(jnp.bfloat16)
    store_mixed = pltpu.make_async_copy(mixed_v, mixed_hbm, store_sem.at[0])
    store_mixed.start()
    dots = jnp.sum(act * cot[...].astype(jnp.float32), axis=1, keepdims=True) * factor
    gate_grad_ref[...] = jnp.transpose(jnp.broadcast_to(dots, (rows, 128)))[0:1, :]

    near_grad.wait()
    for part in range(pieces):
        for j in range(2, n):
            remote(GRAD, grad_out, grad_home, j, part, far_at(part, j), ROWS).wait()
    both = gate * factor
    width = tile_of(depth, 512)
    stores = []
    for i in range(depth // width):
        cut = pl.ds(i * width, width)
        grad_v[:, cut] = (
            jnp.dot(unplace[...], grad_home[:, cut], preferred_element_type=jnp.float32) * both
        ).astype(jnp.bfloat16)
        store = pltpu.make_async_copy(grad_v.at[:, cut], grad_hbm.at[:, cut], store_sem.at[1 + i])
        store.start()
        stores.append(store)
    store_mixed.wait()
    for store in stores:
        store.wait()


def solution(mesh):
    n = mesh.shape["expert"]
    groups = mesh.shape["dp"]

    def shards(tokens, routes, gates, counts, expert_weight, cotangent):
        rows, depth = tokens.shape
        units = cotangent.shape[1]
        cap = -(-(3 * rows // (2 * n)) // ROWS) * ROWS
        slots = n * cap
        pieces = cap // ROWS
        small = max(2 * cap, (n - 2) * ROWS)
        bf16 = jnp.bfloat16
        hbm = pl.BlockSpec(memory_space=pl.ANY)
        vmem = pl.BlockSpec(memory_space=pltpu.VMEM)
        mixed, token_grad, gate_grad = pl.pallas_call(
            functools.partial(kernel, n, groups, cap),
            out_shape=(
                jax.ShapeDtypeStruct((rows, units), bf16),
                jax.ShapeDtypeStruct((rows, depth), bf16),
                jax.ShapeDtypeStruct((1, rows), jnp.float32),
            ),
            in_specs=[vmem, vmem, pl.BlockSpec(memory_space=pltpu.SMEM), hbm, hbm, hbm],
            out_specs=(hbm, hbm, vmem),
            scratch_shapes=[
                pltpu.VMEM((rows, depth), bf16),
                pltpu.VMEM((rows, units), bf16),
                pltpu.VMEM((depth, units), bf16),
                pltpu.VMEM((slots, rows), bf16),
                pltpu.VMEM((rows, slots), bf16),
                pltpu.VMEM((slots, depth), bf16),
                pltpu.VMEM((slots, units), bf16),
                pltpu.VMEM((slots, depth), bf16),
                pltpu.VMEM((slots, units), bf16),
                pltpu.VMEM((small, units), bf16),
                pltpu.VMEM((slots, units), bf16),
                pltpu.VMEM((slots, depth), bf16),
                pltpu.VMEM((slots, units), bf16),
                pltpu.VMEM((slots, depth), bf16),
                pltpu.VMEM((rows, units), bf16),
                pltpu.VMEM((rows, depth), bf16),
                pltpu.VMEM((8, 128), jnp.float32),
                pltpu.VMEM((groups - 1, 8, 128), jnp.float32),
                pltpu.VMEM((8, 128), jnp.float32),
                pltpu.VMEM((n - 1, 8, 128), jnp.float32),
                pltpu.SemaphoreType.DMA((3,)),
                pltpu.SemaphoreType.DMA((1 + depth // tile_of(depth, 512),)),
                pltpu.SemaphoreType.DMA((4, n, pieces)),
                pltpu.SemaphoreType.DMA((4, n, pieces)),
                pltpu.SemaphoreType.DMA((groups - 1 + n - 1,)),
                pltpu.SemaphoreType.DMA((groups - 1 + n - 1,)),
            ],
            compiler_params=pltpu.CompilerParams(
                collective_id=0, has_side_effects=True, vmem_limit_bytes=48 * 1024 * 1024
            ),
        )(routes.reshape(1, rows), gates.reshape(1, rows), counts, tokens, expert_weight, cotangent)
        return (mixed, token_grad, gate_grad.reshape(rows, 1))

    spread = P(("dp", "expert"), None)
    return jax.shard_map(
        shards,
        mesh=mesh,
        in_specs=(spread, spread, spread, P(("dp", "expert")), P("expert", None, None), spread),
        out_specs=(spread, spread, spread),
        check_vma=False,
    )
```

```python
import functools

import jax
import jax.numpy as jnp
from jax import lax
from jax.experimental import pallas as pl
from jax.experimental.pallas import tpu as pltpu
from jax.sharding import PartitionSpec as P

MESH = pl.DeviceIdType.MESH
ROWS = 16
TOK, COT, ACT, GRAD = 0, 1, 2, 3


def tile_of(size, most):
    tile = most
    while size % tile:
        tile //= 2
    return tile


def kernel(
    n, groups, cap, routes_hbm, gates_hbm, counts_ref, tokens_hbm, weight_hbm, cotangent_hbm,
    mixed_hbm, grad_hbm, gate_grad_ref,
    routes_ref, gates_ref, tok, cot, w, place, unplace, tok_out, cot_out, tok_in, cot_in, delta,
    act_out, grad_out, act_home, grad_home, mixed_v, grad_v, cnt_mine, cnt_dp, cnt_sum, cnt_ex,
    load_sem, store_sem, send_sem, recv_sem, cnt_send, cnt_recv,
):
    rows, depth = tok.shape
    units = cot.shape[1]
    slots = n * cap
    pieces = cap // ROWS
    far = n - 2
    step = far * ROWS
    me = lax.axis_index("expert")
    group = lax.axis_index("dp")

    load_tok = pltpu.make_async_copy(tokens_hbm, tok, load_sem.at[0])
    load_cot = pltpu.make_async_copy(cotangent_hbm, cot, load_sem.at[1])
    load_w = pltpu.make_async_copy(weight_hbm.at[0], w, load_sem.at[2])
    load_routes = pltpu.make_async_copy(routes_hbm, routes_ref, load_sem.at[3])
    load_gates = pltpu.make_async_copy(gates_hbm, gates_ref, load_sem.at[4])
    load_routes.start()
    load_gates.start()
    load_tok.start()
    load_cot.start()

    barrier = pltpu.get_barrier_semaphore()
    for j in range(1, n):
        pl.semaphore_signal(
            barrier, inc=1, device_id=(group, lax.bitwise_xor(me, j)), device_id_type=MESH
        )
    for k in range(1, groups):
        pl.semaphore_signal(
            barrier, inc=1, device_id=(lax.rem(group + k, groups), me), device_id_type=MESH
        )

    load_routes.wait()
    load_gates.wait()
    route = routes_ref[...]
    high = -(-n // ROWS) * ROWS
    choose = lax.broadcasted_iota(jnp.int32, (high, rows), 0) == route
    choose_f = jnp.where(choose, 1.0, 0.0)
    upper = jnp.where(
        lax.broadcasted_iota(jnp.int32, (rows, rows), 0)
        <= lax.broadcasted_iota(jnp.int32, (rows, rows), 1),
        1.0,
        0.0,
    ).astype(jnp.bfloat16)
    running = jnp.dot(choose_f.astype(jnp.bfloat16), upper, preferred_element_type=jnp.float32)
    rank = (jnp.sum(running * choose_f, axis=0, keepdims=True) - 1.0).astype(jnp.int32)
    rel = lax.bitwise_xor(route, jnp.full(route.shape, me, jnp.int32))
    piece = lax.div(rank, jnp.int32(ROWS))
    slot = jnp.where(
        rel < 2,
        rel * cap + rank,
        2 * cap + piece * step + (rel - 2) * ROWS + (rank - piece * ROWS),
    )
    place[...] = jnp.where(
        lax.broadcasted_iota(jnp.int32, (slots, rows), 0) == slot, 1.0, 0.0
    ).astype(jnp.bfloat16)
    line = lax.broadcasted_iota(jnp.int32, (128, rows), 0)
    columns = jnp.transpose(
        jnp.where(line == 0, gates_ref[...], jnp.where(line == 1, slot.astype(jnp.float32), 0.0))
    )
    gate = columns[:, 0:1]
    unplace[...] = jnp.where(
        lax.broadcasted_iota(jnp.int32, (rows, slots), 1) == columns[:, 1:2].astype(jnp.int32),
        1.0,
        0.0,
    ).astype(jnp.bfloat16)
    count = counts_ref[0]
    cnt_mine[...] = jnp.full(cnt_mine.shape, count.astype(jnp.float32), jnp.float32)

    def remote(kind, source, target, j, part, at, size):
        return pltpu.make_async_remote_copy(
            src_ref=source.at[pl.ds(at, size)],
            dst_ref=target.at[pl.ds(at, size)],
            send_sem=send_sem.at[kind, j, part],
            recv_sem=recv_sem.at[kind, j, part],
            device_id=(group, lax.bitwise_xor(me, j)),
            device_id_type=MESH,
        )

    def gather(source, target, at, size):
        width = tile_of(source.shape[1], 512)

        def body(i, carry):
            cut = pl.ds(pl.multiple_of(i * width, width), width)
            target[at : at + size, cut] = jnp.dot(
                place[at : at + size, :], source[:, cut], preferred_element_type=jnp.float32
            ).astype(jnp.bfloat16)
            return carry

        lax.fori_loop(0, source.shape[1] // width, body, 0)

    def far_at(part, j):
        return 2 * cap + part * step + (j - 2) * ROWS

    out = []

    def send_far(part):
        gather(tok, tok_out, 2 * cap + part * step, step)
        if part == 0:
            pl.semaphore_wait(barrier, n - 1 + groups - 1)
        for j in range(2, n):
            copy = remote(TOK, tok_out, tok_in, j, part, far_at(part, j), ROWS)
            copy.start()
            out.append(copy)
        if part == 0:
            load_cot.wait()
            load_w.start()
        gather(cot, cot_out, 2 * cap + part * step, step)
        for j in range(2, n):
            copy = remote(COT, cot_out, cot_in, j, part, far_at(part, j), ROWS)
            copy.start()
            out.append(copy)

    early = min(2, pieces)
    load_tok.wait()
    send_far(0)
    gather(tok, tok_out, cap, cap)
    near_tok = remote(TOK, tok_out, tok_in, 1, 0, cap, cap)
    near_tok.start()
    gather(cot, cot_out, cap, cap)
    near_cot = remote(COT, cot_out, cot_in, 1, 0, cap, cap)
    near_cot.start()
    for part in range(1, early):
        send_far(part)

    counts = []
    for k in range(1, groups):
        copy = pltpu.make_async_remote_copy(
            src_ref=cnt_mine,
            dst_ref=cnt_dp.at[k - 1],
            send_sem=cnt_send.at[k - 1],
            recv_sem=cnt_recv.at[k - 1],
            device_id=(lax.rem(group + k, groups), me),
            device_id_type=MESH,
        )
        copy.start()
        counts.append(copy)

    gather(tok, tok_in, 0, cap)
    gather(cot, cot_in, 0, cap)

    def forward(at, size, kept):
        width = tile_of(units, 256)

        def body(i, carry):
            cut = pl.ds(pl.multiple_of(i * width, width), width)
            pre = jnp.dot(
                tok_in[at : at + size, :], w[:, cut], preferred_element_type=jnp.float32
            )
            sig = jax.nn.sigmoid(pre)
            act = (pre * sig).astype(jnp.bfloat16)
            if kept:
                act_home[at : at + kept, cut] = act[:kept]
            act_out[at + kept : at + size, cut] = act[kept:]
            slope = sig * (1.0 + pre * (1.0 - sig))
            delta[0:size, cut] = (
                cot_in[at : at + size, cut].astype(jnp.float32) * slope
            ).astype(jnp.bfloat16)
            return carry

        lax.fori_loop(0, units // width, body, 0)

    def backward(at, size, kept):
        width = tile_of(depth, 512)

        def body(i, carry):
            cut = pl.ds(pl.multiple_of(i * width, width), width)
            grad = lax.dot_general(
                delta[0:size, :], w[cut, :], (((1,), (1,)), ((), ())),
                preferred_element_type=jnp.float32,
            ).astype(jnp.bfloat16)
            if kept:
                grad_home[at : at + kept, cut] = grad[:kept]
            grad_out[at + kept : at + size, cut] = grad[kept:]
            return carry

        lax.fori_loop(0, depth // width, body, 0)

    load_w.wait()
    near_tok.wait_recv()
    near_cot.wait_recv()
    forward(0, 2 * cap, cap)
    near_act = remote(ACT, act_out, act_home, 1, 0, cap, cap)
    near_act.start()
    backward(0, 2 * cap, cap)
    near_grad = remote(GRAD, grad_out, grad_home, 1, 0, cap, cap)
    near_grad.start()
    for part in range(early, pieces):
        send_far(part)

    for copy in counts:
        copy.wait_recv()
    partial = cnt_mine[...]
    for k in range(1, groups):
        partial = partial + cnt_dp[k - 1]
    cnt_sum[...] = partial
    sums = []
    for j in range(1, n):
        copy = pltpu.make_async_remote_copy(
            src_ref=cnt_sum,
            dst_ref=cnt_ex.at[j - 1],
            send_sem=cnt_send.at[groups - 1 + j - 1],
            recv_sem=cnt_recv.at[groups - 1 + j - 1],
            device_id=(group, lax.bitwise_xor(me, j)),
            device_id_type=MESH,
        )
        copy.start()
        sums.append(copy)

    for part in range(pieces):
        at = 2 * cap + part * step
        for kind in (TOK, COT):
            for j in range(2, n):
                if kind == TOK:
                    remote(TOK, tok_out, tok_in, j, part, far_at(part, j), ROWS).wait_recv()
                else:
                    remote(COT, cot_out, cot_in, j, part, far_at(part, j), ROWS).wait_recv()
        forward(at, step, 0)
        for j in range(2, n):
            copy = remote(ACT, act_out, act_home, j, part, far_at(part, j), ROWS)
            copy.start()
        backward(at, step, 0)
        for j in range(2, n):
            copy = remote(GRAD, grad_out, grad_home, j, part, far_at(part, j), ROWS)
            copy.start()

    for copy in out:
        copy.wait_send()
    near_tok.wait_send()
    near_cot.wait_send()
    for copy in counts:
        copy.wait_send()
    for copy in sums:
        copy.wait()
    total = partial
    for j in range(1, n):
        total = total + cnt_ex[j - 1]
    scale = jnp.float32(rows * groups * n) / total[0:1, 0:1]
    position = lax.broadcasted_iota(jnp.int32, (rows, 1), 0)
    factor = jnp.where(position < count, 1.0, 0.0) * scale

    near_act.wait()
    for part in range(pieces):
        for j in range(2, n):
            remote(ACT, act_out, act_home, j, part, far_at(part, j), ROWS).wait()
    act = jnp.dot(unplace[...], act_home[...], preferred_element_type=jnp.float32)
    mixed_v[...] = (gate * act).astype(jnp.bfloat16)
    store_mixed = pltpu.make_async_copy(mixed_v, mixed_hbm, store_sem.at[0])
    store_mixed.start()
    dots = jnp.sum(act * cot[...].astype(jnp.float32), axis=1, keepdims=True) * factor
    gate_grad_ref[...] = jnp.transpose(jnp.broadcast_to(dots, (rows, 128)))[0:1, :]

    near_grad.wait()
    for part in range(pieces):
        for j in range(2, n):
            remote(GRAD, grad_out, grad_home, j, part, far_at(part, j), ROWS).wait()
    both = gate * factor
    width = tile_of(depth, 512)
    stores = []
    for i in range(depth // width):
        cut = pl.ds(i * width, width)
        grad_v[:, cut] = (
            jnp.dot(unplace[...], grad_home[:, cut], preferred_element_type=jnp.float32) * both
        ).astype(jnp.bfloat16)
        store = pltpu.make_async_copy(grad_v.at[:, cut], grad_hbm.at[:, cut], store_sem.at[1 + i])
        store.start()
        stores.append(store)
    store_mixed.wait()
    for store in stores:
        store.wait()


def solution(mesh):
    n = mesh.shape["expert"]
    groups = mesh.shape["dp"]

    def shards(tokens, routes, gates, counts, expert_weight, cotangent):
        rows, depth = tokens.shape
        units = cotangent.shape[1]
        cap = -(-(3 * rows // (2 * n)) // ROWS) * ROWS
        slots = n * cap
        pieces = cap // ROWS
        small = max(2 * cap, (n - 2) * ROWS)
        bf16 = jnp.bfloat16
        hbm = pl.BlockSpec(memory_space=pl.ANY)
        vmem = pl.BlockSpec(memory_space=pltpu.VMEM)
        mixed, token_grad, gate_grad = pl.pallas_call(
            functools.partial(kernel, n, groups, cap),
            out_shape=(
                jax.ShapeDtypeStruct((rows, units), bf16),
                jax.ShapeDtypeStruct((rows, depth), bf16),
                jax.ShapeDtypeStruct((1, rows), jnp.float32),
            ),
            in_specs=[hbm, hbm, pl.BlockSpec(memory_space=pltpu.SMEM), hbm, hbm, hbm],
            out_specs=(hbm, hbm, vmem),
            scratch_shapes=[
                pltpu.VMEM((1, rows), jnp.int32),
                pltpu.VMEM((1, rows), jnp.float32),
                pltpu.VMEM((rows, depth), bf16),
                pltpu.VMEM((rows, units), bf16),
                pltpu.VMEM((depth, units), bf16),
                pltpu.VMEM((slots, rows), bf16),
                pltpu.VMEM((rows, slots), bf16),
                pltpu.VMEM((slots, depth), bf16),
                pltpu.VMEM((slots, units), bf16),
                pltpu.VMEM((slots, depth), bf16),
                pltpu.VMEM((slots, units), bf16),
                pltpu.VMEM((small, units), bf16),
                pltpu.VMEM((slots, units), bf16),
                pltpu.VMEM((slots, depth), bf16),
                pltpu.VMEM((slots, units), bf16),
                pltpu.VMEM((slots, depth), bf16),
                pltpu.VMEM((rows, units), bf16),
                pltpu.VMEM((rows, depth), bf16),
                pltpu.VMEM((8, 128), jnp.float32),
                pltpu.VMEM((groups - 1, 8, 128), jnp.float32),
                pltpu.VMEM((8, 128), jnp.float32),
                pltpu.VMEM((n - 1, 8, 128), jnp.float32),
                pltpu.SemaphoreType.DMA((5,)),
                pltpu.SemaphoreType.DMA((1 + depth // tile_of(depth, 512),)),
                pltpu.SemaphoreType.DMA((4, n, pieces)),
                pltpu.SemaphoreType.DMA((4, n, pieces)),
                pltpu.SemaphoreType.DMA((groups - 1 + n - 1,)),
                pltpu.SemaphoreType.DMA((groups - 1 + n - 1,)),
            ],
            compiler_params=pltpu.CompilerParams(
                collective_id=0, has_side_effects=True, vmem_limit_bytes=63 * 1024 * 1024
            ),
        )(routes.reshape(1, rows), gates.reshape(1, rows), counts, tokens, expert_weight, cotangent)
        return (mixed, token_grad, gate_grad.reshape(rows, 1))

    spread = P(("dp", "expert"), None)
    return jax.shard_map(
        shards,
        mesh=mesh,
        in_specs=(spread, spread, spread, P(("dp", "expert")), P("expert", None, None), spread),
        out_specs=(spread, spread, spread),
        check_vma=False,
    )
```

```python
import functools

import jax
import jax.numpy as jnp
from jax import lax
from jax.experimental import pallas as pl
from jax.experimental.pallas import tpu as pltpu
from jax.sharding import PartitionSpec as P

MESH = pl.DeviceIdType.MESH
ROWS = 16
TOK, COT, ACT, GRAD = 0, 1, 2, 3


def tile_of(size, most):
    tile = most
    while size % tile:
        tile //= 2
    return tile


def kernel(
    n, groups, cap, routes_hbm, gates_hbm, counts_ref, tokens_hbm, weight_hbm, cotangent_hbm,
    act_home, grad_home, unplace, columns_ref,
    routes_ref, gates_ref, tok, cot, w, place, tok_out, cot_out, tok_in, cot_in, delta,
    act_out, grad_out, cnt_mine, cnt_dp, cnt_sum, cnt_ex,
    load_sem, send_sem, recv_sem, cnt_send, cnt_recv,
):
    rows, depth = tok.shape
    units = cot.shape[1]
    slots = n * cap
    pieces = cap // ROWS
    far = n - 2
    step = far * ROWS
    me = lax.axis_index("expert")
    group = lax.axis_index("dp")

    load_tok = pltpu.make_async_copy(tokens_hbm, tok, load_sem.at[0])
    load_cot = pltpu.make_async_copy(cotangent_hbm, cot, load_sem.at[1])
    load_w = pltpu.make_async_copy(weight_hbm.at[0], w, load_sem.at[2])
    load_routes = pltpu.make_async_copy(routes_hbm, routes_ref, load_sem.at[3])
    load_gates = pltpu.make_async_copy(gates_hbm, gates_ref, load_sem.at[4])
    load_routes.start()
    load_gates.start()
    load_tok.start()
    load_cot.start()

    barrier = pltpu.get_barrier_semaphore()
    for j in range(1, n):
        pl.semaphore_signal(
            barrier, inc=1, device_id=(group, lax.bitwise_xor(me, j)), device_id_type=MESH
        )
    for k in range(1, groups):
        pl.semaphore_signal(
            barrier, inc=1, device_id=(lax.rem(group + k, groups), me), device_id_type=MESH
        )

    load_routes.wait()
    load_gates.wait()
    route = routes_ref[...]
    high = -(-n // ROWS) * ROWS
    choose = lax.broadcasted_iota(jnp.int32, (high, rows), 0) == route
    choose_f = jnp.where(choose, 1.0, 0.0)
    upper = jnp.where(
        lax.broadcasted_iota(jnp.int32, (rows, rows), 0)
        <= lax.broadcasted_iota(jnp.int32, (rows, rows), 1),
        1.0,
        0.0,
    ).astype(jnp.bfloat16)
    running = jnp.dot(choose_f.astype(jnp.bfloat16), upper, preferred_element_type=jnp.float32)
    rank = (jnp.sum(running * choose_f, axis=0, keepdims=True) - 1.0).astype(jnp.int32)
    rel = lax.bitwise_xor(route, jnp.full(route.shape, me, jnp.int32))
    piece = lax.div(rank, jnp.int32(ROWS))
    slot = jnp.where(
        rel < 2,
        rel * cap + rank,
        2 * cap + piece * step + (rel - 2) * ROWS + (rank - piece * ROWS),
    )
    place[...] = jnp.where(
        lax.broadcasted_iota(jnp.int32, (slots, rows), 0) == slot, 1.0, 0.0
    ).astype(jnp.bfloat16)
    line = lax.broadcasted_iota(jnp.int32, (128, rows), 0)
    columns = jnp.transpose(
        jnp.where(line == 0, gates_ref[...], jnp.where(line == 1, slot.astype(jnp.float32), 0.0))
    )
    gate = columns[:, 0:1]
    unplace[...] = jnp.where(
        lax.broadcasted_iota(jnp.int32, (rows, slots), 1) == columns[:, 1:2].astype(jnp.int32),
        1.0,
        0.0,
    ).astype(jnp.bfloat16)
    count = counts_ref[0]
    cnt_mine[...] = jnp.full(cnt_mine.shape, count.astype(jnp.float32), jnp.float32)

    def remote(kind, source, target, j, part, at, size):
        return pltpu.make_async_remote_copy(
            src_ref=source.at[pl.ds(at, size)],
            dst_ref=target.at[pl.ds(at, size)],
            send_sem=send_sem.at[kind, j, part],
            recv_sem=recv_sem.at[kind, j, part],
            device_id=(group, lax.bitwise_xor(me, j)),
            device_id_type=MESH,
        )

    def gather(source, target, at, size):
        width = tile_of(source.shape[1], 512)

        def body(i, carry):
            cut = pl.ds(pl.multiple_of(i * width, width), width)
            target[at : at + size, cut] = jnp.dot(
                place[at : at + size, :], source[:, cut], preferred_element_type=jnp.float32
            ).astype(jnp.bfloat16)
            return carry

        lax.fori_loop(0, source.shape[1] // width, body, 0)

    def far_at(part, j):
        return 2 * cap + part * step + (j - 2) * ROWS

    out = []

    def send_far(part):
        gather(tok, tok_out, 2 * cap + part * step, step)
        if part == 0:
            pl.semaphore_wait(barrier, n - 1 + groups - 1)
        for j in range(2, n):
            copy = remote(TOK, tok_out, tok_in, j, part, far_at(part, j), ROWS)
            copy.start()
            out.append(copy)
        if part == 0:
            load_cot.wait()
            load_w.start()
        gather(cot, cot_out, 2 * cap + part * step, step)
        for j in range(2, n):
            copy = remote(COT, cot_out, cot_in, j, part, far_at(part, j), ROWS)
            copy.start()
            out.append(copy)

    early = min(2, pieces)
    load_tok.wait()
    send_far(0)
    gather(tok, tok_out, cap, cap)
    near_tok = remote(TOK, tok_out, tok_in, 1, 0, cap, cap)
    near_tok.start()
    gather(cot, cot_out, cap, cap)
    near_cot = remote(COT, cot_out, cot_in, 1, 0, cap, cap)
    near_cot.start()
    for part in range(1, early):
        send_far(part)

    counts = []
    for k in range(1, groups):
        copy = pltpu.make_async_remote_copy(
            src_ref=cnt_mine,
            dst_ref=cnt_dp.at[k - 1],
            send_sem=cnt_send.at[k - 1],
            recv_sem=cnt_recv.at[k - 1],
            device_id=(lax.rem(group + k, groups), me),
            device_id_type=MESH,
        )
        copy.start()
        counts.append(copy)

    gather(tok, tok_in, 0, cap)
    gather(cot, cot_in, 0, cap)

    def forward(at, size):
        width = tile_of(units, 256)

        def body(i, carry):
            cut = pl.ds(pl.multiple_of(i * width, width), width)
            pre = jnp.dot(
                tok_in[at : at + size, :], w[:, cut], preferred_element_type=jnp.float32
            )
            sig = jax.nn.sigmoid(pre)
            act = (pre * sig).astype(jnp.bfloat16)
            act_out[at : at + size, cut] = act
            slope = sig * (1.0 + pre * (1.0 - sig))
            delta[0:size, cut] = (
                cot_in[at : at + size, cut].astype(jnp.float32) * slope
            ).astype(jnp.bfloat16)
            return carry

        lax.fori_loop(0, units // width, body, 0)

    def backward(at, size):
        width = tile_of(depth, 512)

        def body(i, carry):
            cut = pl.ds(pl.multiple_of(i * width, width), width)
            grad = lax.dot_general(
                delta[0:size, :], w[cut, :], (((1,), (1,)), ((), ())),
                preferred_element_type=jnp.float32,
            ).astype(jnp.bfloat16)
            grad_out[at : at + size, cut] = grad
            return carry

        lax.fori_loop(0, depth // width, body, 0)

    load_w.wait()
    near_tok.wait_recv()
    near_cot.wait_recv()
    forward(0, 2 * cap)
    near_act = remote(ACT, act_out, act_home, 1, 0, cap, cap)
    near_act.start()
    own_act = pltpu.make_async_copy(
        act_out.at[pl.ds(0, cap)], act_home.at[pl.ds(0, cap)], load_sem.at[0]
    )
    own_act.start()
    backward(0, 2 * cap)
    near_grad = remote(GRAD, grad_out, grad_home, 1, 0, cap, cap)
    near_grad.start()
    own_grad = pltpu.make_async_copy(
        grad_out.at[pl.ds(0, cap)], grad_home.at[pl.ds(0, cap)], load_sem.at[1]
    )
    own_grad.start()
    for part in range(early, pieces):
        send_far(part)

    for copy in counts:
        copy.wait_recv()
    partial = cnt_mine[...]
    for k in range(1, groups):
        partial = partial + cnt_dp[k - 1]
    cnt_sum[...] = partial
    sums = []
    for j in range(1, n):
        copy = pltpu.make_async_remote_copy(
            src_ref=cnt_sum,
            dst_ref=cnt_ex.at[j - 1],
            send_sem=cnt_send.at[groups - 1 + j - 1],
            recv_sem=cnt_recv.at[groups - 1 + j - 1],
            device_id=(group, lax.bitwise_xor(me, j)),
            device_id_type=MESH,
        )
        copy.start()
        sums.append(copy)

    for part in range(pieces):
        at = 2 * cap + part * step
        for kind in (TOK, COT):
            for j in range(2, n):
                if kind == TOK:
                    remote(TOK, tok_out, tok_in, j, part, far_at(part, j), ROWS).wait_recv()
                else:
                    remote(COT, cot_out, cot_in, j, part, far_at(part, j), ROWS).wait_recv()
        forward(at, step)
        for j in range(2, n):
            copy = remote(ACT, act_out, act_home, j, part, far_at(part, j), ROWS)
            copy.start()
        backward(at, step)
        for j in range(2, n):
            copy = remote(GRAD, grad_out, grad_home, j, part, far_at(part, j), ROWS)
            copy.start()

    for copy in out:
        copy.wait_send()
    near_tok.wait_send()
    near_cot.wait_send()
    for copy in counts:
        copy.wait_send()
    for copy in sums:
        copy.wait()
    total = partial
    for j in range(1, n):
        total = total + cnt_ex[j - 1]
    scale = jnp.float32(rows * groups * n) / total[0:1, 0:1]
    position = lax.broadcasted_iota(jnp.int32, (rows, 1), 0)
    factor = jnp.where(position < count, 1.0, 0.0) * scale

    lane = lax.broadcasted_iota(jnp.int32, (rows, 128), 1)
    columns_ref[...] = jnp.where(
        lane == 0, gate, jnp.where(lane == 1, gate * factor, factor)
    )

    own_act.wait()
    own_grad.wait()
    near_act.wait()
    near_grad.wait()
    for part in range(pieces):
        for j in range(2, n):
            remote(ACT, act_out, act_home, j, part, far_at(part, j), ROWS).wait()
            remote(GRAD, grad_out, grad_home, j, part, far_at(part, j), ROWS).wait()


def finish(
    act_home, grad_home, unplace, columns, cotangent_hbm,
    mixed_hbm, grad_hbm, gate_grad_ref, cot, mixed_v, grad_v, load_sem, store_sem,
):
    rows, depth = grad_v.shape
    load_cot = pltpu.make_async_copy(cotangent_hbm, cot, load_sem.at[0])
    load_cot.start()
    both = columns[:, 1:2]
    width = tile_of(depth, 512)
    stores = []
    for i in range(depth // width):
        cut = pl.ds(i * width, width)
        grad_v[:, cut] = (
            jnp.dot(unplace[...], grad_home[:, cut], preferred_element_type=jnp.float32) * both
        ).astype(jnp.bfloat16)
        store = pltpu.make_async_copy(grad_v.at[:, cut], grad_hbm.at[:, cut], store_sem.at[1 + i])
        store.start()
        stores.append(store)
    act = jnp.dot(unplace[...], act_home[...], preferred_element_type=jnp.float32)
    mixed_v[...] = (columns[:, 0:1] * act).astype(jnp.bfloat16)
    store_mixed = pltpu.make_async_copy(mixed_v, mixed_hbm, store_sem.at[0])
    store_mixed.start()
    load_cot.wait()
    dots = jnp.sum(act * cot[...].astype(jnp.float32), axis=1, keepdims=True) * columns[:, 2:3]
    gate_grad_ref[...] = jnp.transpose(jnp.broadcast_to(dots, (rows, 128)))[0:1, :]
    store_mixed.wait()
    for store in stores:
        store.wait()


def pinned(array):
    return pltpu.with_memory_space_constraint(array, pltpu.HBM)


def solution(mesh):
    n = mesh.shape["expert"]
    groups = mesh.shape["dp"]

    def shards(tokens, routes, gates, counts, expert_weight, cotangent):
        rows, depth = tokens.shape
        units = cotangent.shape[1]
        cap = -(-(3 * rows // (2 * n)) // ROWS) * ROWS
        slots = n * cap
        pieces = cap // ROWS
        small = max(2 * cap, (n - 2) * ROWS)
        bf16 = jnp.bfloat16
        hbm = pl.BlockSpec(memory_space=pltpu.HBM)
        held = pinned(cotangent)
        free = pl.BlockSpec(memory_space=pl.ANY)
        vmem = pl.BlockSpec(memory_space=pltpu.VMEM)
        act_home, grad_home, unplace, columns = pl.pallas_call(
            functools.partial(kernel, n, groups, cap),
            out_shape=(
                jax.ShapeDtypeStruct((slots, units), bf16),
                jax.ShapeDtypeStruct((slots, depth), bf16),
                jax.ShapeDtypeStruct((rows, slots), bf16),
                jax.ShapeDtypeStruct((rows, 128), jnp.float32),
            ),
            in_specs=[hbm, hbm, pl.BlockSpec(memory_space=pltpu.SMEM), hbm, hbm, hbm],
            out_specs=(free, free, vmem, vmem),
            scratch_shapes=[
                pltpu.VMEM((1, rows), jnp.int32),
                pltpu.VMEM((1, rows), jnp.float32),
                pltpu.VMEM((rows, depth), bf16),
                pltpu.VMEM((rows, units), bf16),
                pltpu.VMEM((depth, units), bf16),
                pltpu.VMEM((slots, rows), bf16),
                pltpu.VMEM((slots, depth), bf16),
                pltpu.VMEM((slots, units), bf16),
                pltpu.VMEM((slots, depth), bf16),
                pltpu.VMEM((slots, units), bf16),
                pltpu.VMEM((small, units), bf16),
                pltpu.VMEM((slots, units), bf16),
                pltpu.VMEM((slots, depth), bf16),
                pltpu.VMEM((8, 128), jnp.float32),
                pltpu.VMEM((groups - 1, 8, 128), jnp.float32),
                pltpu.VMEM((8, 128), jnp.float32),
                pltpu.VMEM((n - 1, 8, 128), jnp.float32),
                pltpu.SemaphoreType.DMA((5,)),
                pltpu.SemaphoreType.DMA((4, n, pieces)),
                pltpu.SemaphoreType.DMA((4, n, pieces)),
                pltpu.SemaphoreType.DMA((groups - 1 + n - 1,)),
                pltpu.SemaphoreType.DMA((groups - 1 + n - 1,)),
            ],
            compiler_params=pltpu.CompilerParams(
                collective_id=0, has_side_effects=True, vmem_limit_bytes=40 * 1024 * 1024
            ),
        )(
            pinned(routes.reshape(1, rows)),
            pinned(gates.reshape(1, rows)),
            counts,
            pinned(tokens),
            pinned(expert_weight),
            held,
        )
        mixed, token_grad, gate_grad = pl.pallas_call(
            finish,
            out_shape=(
                jax.ShapeDtypeStruct((rows, units), bf16),
                jax.ShapeDtypeStruct((rows, depth), bf16),
                jax.ShapeDtypeStruct((1, rows), jnp.float32),
            ),
            in_specs=[vmem, vmem, vmem, vmem, hbm],
            out_specs=(hbm, hbm, vmem),
            scratch_shapes=[
                pltpu.VMEM((rows, units), bf16),
                pltpu.VMEM((rows, units), bf16),
                pltpu.VMEM((rows, depth), bf16),
                pltpu.SemaphoreType.DMA((1,)),
                pltpu.SemaphoreType.DMA((1 + depth // tile_of(depth, 512),)),
            ],
            compiler_params=pltpu.CompilerParams(vmem_limit_bytes=24 * 1024 * 1024),
        )(act_home, grad_home, unplace, columns, held)
        return (mixed, token_grad, gate_grad.reshape(rows, 1))

    spread = P(("dp", "expert"), None)
    return jax.shard_map(
        shards,
        mesh=mesh,
        in_specs=(spread, spread, spread, P(("dp", "expert")), P("expert", None, None), spread),
        out_specs=(spread, spread, spread),
        check_vma=False,
    )
```

```python
import functools

import jax
import jax.numpy as jnp
from jax import lax
from jax.experimental import pallas as pl
from jax.experimental.pallas import tpu as pltpu
from jax.sharding import PartitionSpec as P

MESH = pl.DeviceIdType.MESH
ROWS = 16
TOK, COT, ACT, GRAD = 0, 1, 2, 3


def tile_of(size, most):
    tile = most
    while size % tile:
        tile //= 2
    return tile


def kernel(
    n, groups, cap, routes_hbm, gates_hbm, counts_ref, tokens_hbm, weight_hbm, cotangent_hbm,
    mixed_ref, gate_grad_ref, grad_home, unplace, columns_ref,
    routes_ref, gates_ref, tok, cot, w, place, tok_out, cot_out, tok_in, cot_in, delta,
    act_out, act_home, grad_out, cnt_mine, cnt_dp, cnt_sum, cnt_ex,
    load_sem, send_sem, recv_sem, cnt_send, cnt_recv,
):
    rows, depth = tok.shape
    units = cot.shape[1]
    slots = n * cap
    pieces = cap // ROWS
    far = n - 2
    step = far * ROWS
    me = lax.axis_index("expert")
    group = lax.axis_index("dp")

    barrier = pltpu.get_barrier_semaphore()
    for j in range(1, n):
        pl.semaphore_signal(
            barrier, inc=1, device_id=(group, lax.bitwise_xor(me, j)), device_id_type=MESH
        )
    for k in range(1, groups):
        pl.semaphore_signal(
            barrier, inc=1, device_id=(lax.rem(group + k, groups), me), device_id_type=MESH
        )

    load_tok = pltpu.make_async_copy(tokens_hbm, tok, load_sem.at[0])
    load_cot = pltpu.make_async_copy(cotangent_hbm, cot, load_sem.at[1])
    load_w = pltpu.make_async_copy(weight_hbm.at[0], w, load_sem.at[2])
    load_routes = pltpu.make_async_copy(routes_hbm, routes_ref, load_sem.at[3])
    load_gates = pltpu.make_async_copy(gates_hbm, gates_ref, load_sem.at[4])
    load_routes.start()
    load_gates.start()
    load_tok.start()
    load_cot.start()

    load_routes.wait()
    load_gates.wait()
    route = routes_ref[...]
    high = -(-n // ROWS) * ROWS
    choose = lax.broadcasted_iota(jnp.int32, (high, rows), 0) == route
    choose_f = jnp.where(choose, 1.0, 0.0)
    upper = jnp.where(
        lax.broadcasted_iota(jnp.int32, (rows, rows), 0)
        <= lax.broadcasted_iota(jnp.int32, (rows, rows), 1),
        1.0,
        0.0,
    ).astype(jnp.bfloat16)
    running = jnp.dot(choose_f.astype(jnp.bfloat16), upper, preferred_element_type=jnp.float32)
    rank = (jnp.sum(running * choose_f, axis=0, keepdims=True) - 1.0).astype(jnp.int32)
    rel = lax.bitwise_xor(route, jnp.full(route.shape, me, jnp.int32))
    piece = lax.div(rank, jnp.int32(ROWS))
    slot = jnp.where(
        rel < 2,
        rel * cap + rank,
        2 * cap + piece * step + (rel - 2) * ROWS + (rank - piece * ROWS),
    )
    place[...] = jnp.where(
        lax.broadcasted_iota(jnp.int32, (slots, rows), 0) == slot, 1.0, 0.0
    ).astype(jnp.bfloat16)
    line = lax.broadcasted_iota(jnp.int32, (128, rows), 0)
    columns = jnp.transpose(
        jnp.where(line == 0, gates_ref[...], jnp.where(line == 1, slot.astype(jnp.float32), 0.0))
    )
    gate = columns[:, 0:1]
    unplace[...] = jnp.where(
        lax.broadcasted_iota(jnp.int32, (rows, slots), 1) == columns[:, 1:2].astype(jnp.int32),
        1.0,
        0.0,
    ).astype(jnp.bfloat16)
    count = counts_ref[0]
    cnt_mine[...] = jnp.full(cnt_mine.shape, count.astype(jnp.float32), jnp.float32)

    def remote(kind, source, target, j, part, at, size):
        return pltpu.make_async_remote_copy(
            src_ref=source.at[pl.ds(at, size)],
            dst_ref=target.at[pl.ds(at, size)],
            send_sem=send_sem.at[kind, j, part],
            recv_sem=recv_sem.at[kind, j, part],
            device_id=(group, lax.bitwise_xor(me, j)),
            device_id_type=MESH,
        )

    def gather(source, target, at, size):
        width = tile_of(source.shape[1], 512)

        def body(i, carry):
            cut = pl.ds(pl.multiple_of(i * width, width), width)
            target[at : at + size, cut] = jnp.dot(
                place[at : at + size, :], source[:, cut], preferred_element_type=jnp.float32
            ).astype(jnp.bfloat16)
            return carry

        lax.fori_loop(0, source.shape[1] // width, body, 0)

    def far_at(part, j):
        return 2 * cap + part * step + (j - 2) * ROWS

    out = []

    def send_far(part):
        gather(tok, tok_out, 2 * cap + part * step, step)
        if part == 0:
            pl.semaphore_wait(barrier, n - 1 + groups - 1)
        for j in range(2, n):
            copy = remote(TOK, tok_out, tok_in, j, part, far_at(part, j), ROWS)
            copy.start()
            out.append(copy)
        if part == 0:
            load_cot.wait()
            load_w.start()
        gather(cot, cot_out, 2 * cap + part * step, step)
        for j in range(2, n):
            copy = remote(COT, cot_out, cot_in, j, part, far_at(part, j), ROWS)
            copy.start()
            out.append(copy)

    early = min(2, pieces)
    load_tok.wait()
    send_far(0)
    gather(tok, tok_out, cap, cap)
    near_tok = remote(TOK, tok_out, tok_in, 1, 0, cap, cap)
    near_tok.start()
    gather(cot, cot_out, cap, cap)
    near_cot = remote(COT, cot_out, cot_in, 1, 0, cap, cap)
    near_cot.start()
    for part in range(1, early):
        send_far(part)

    counts = []
    for k in range(1, groups):
        copy = pltpu.make_async_remote_copy(
            src_ref=cnt_mine,
            dst_ref=cnt_dp.at[k - 1],
            send_sem=cnt_send.at[k - 1],
            recv_sem=cnt_recv.at[k - 1],
            device_id=(lax.rem(group + k, groups), me),
            device_id_type=MESH,
        )
        copy.start()
        counts.append(copy)

    gather(tok, tok_in, 0, cap)
    gather(cot, cot_in, 0, cap)

    def forward(at, size):
        width = tile_of(units, 256)

        def body(i, carry):
            cut = pl.ds(pl.multiple_of(i * width, width), width)
            pre = jnp.dot(
                tok_in[at : at + size, :], w[:, cut], preferred_element_type=jnp.float32
            )
            sig = jax.nn.sigmoid(pre)
            act = (pre * sig).astype(jnp.bfloat16)
            act_out[at : at + size, cut] = act
            slope = sig * (1.0 + pre * (1.0 - sig))
            delta[0:size, cut] = (
                cot_in[at : at + size, cut].astype(jnp.float32) * slope
            ).astype(jnp.bfloat16)
            return carry

        lax.fori_loop(0, units // width, body, 0)

    def backward(at, size):
        width = tile_of(depth, 512)

        def body(i, carry):
            cut = pl.ds(pl.multiple_of(i * width, width), width)
            grad = lax.dot_general(
                delta[0:size, :], w[cut, :], (((1,), (1,)), ((), ())),
                preferred_element_type=jnp.float32,
            ).astype(jnp.bfloat16)
            grad_out[at : at + size, cut] = grad
            return carry

        lax.fori_loop(0, depth // width, body, 0)

    load_w.wait()
    near_tok.wait_recv()
    near_cot.wait_recv()
    forward(0, 2 * cap)
    near_act = remote(ACT, act_out, act_home, 1, 0, cap, cap)
    near_act.start()
    own_act = pltpu.make_async_copy(
        act_out.at[pl.ds(0, cap)], act_home.at[pl.ds(0, cap)], load_sem.at[0]
    )
    own_act.start()
    backward(0, 2 * cap)
    near_grad = remote(GRAD, grad_out, grad_home, 1, 0, cap, cap)
    near_grad.start()
    own_grad = pltpu.make_async_copy(
        grad_out.at[pl.ds(0, cap)], grad_home.at[pl.ds(0, cap)], load_sem.at[1]
    )
    own_grad.start()
    for part in range(early, pieces):
        send_far(part)

    for copy in counts:
        copy.wait_recv()
    partial = cnt_mine[...]
    for k in range(1, groups):
        partial = partial + cnt_dp[k - 1]
    cnt_sum[...] = partial
    sums = []
    for j in range(1, n):
        copy = pltpu.make_async_remote_copy(
            src_ref=cnt_sum,
            dst_ref=cnt_ex.at[j - 1],
            send_sem=cnt_send.at[groups - 1 + j - 1],
            recv_sem=cnt_recv.at[groups - 1 + j - 1],
            device_id=(group, lax.bitwise_xor(me, j)),
            device_id_type=MESH,
        )
        copy.start()
        sums.append(copy)

    for part in range(pieces):
        at = 2 * cap + part * step
        for kind in (TOK, COT):
            for j in range(2, n):
                if kind == TOK:
                    remote(TOK, tok_out, tok_in, j, part, far_at(part, j), ROWS).wait_recv()
                else:
                    remote(COT, cot_out, cot_in, j, part, far_at(part, j), ROWS).wait_recv()
        forward(at, step)
        for j in range(2, n):
            copy = remote(ACT, act_out, act_home, j, part, far_at(part, j), ROWS)
            copy.start()
        backward(at, step)
        for j in range(2, n):
            copy = remote(GRAD, grad_out, grad_home, j, part, far_at(part, j), ROWS)
            copy.start()

    for copy in out:
        copy.wait_send()
    near_tok.wait_send()
    near_cot.wait_send()
    for copy in counts:
        copy.wait_send()
    for copy in sums:
        copy.wait()
    total = partial
    for j in range(1, n):
        total = total + cnt_ex[j - 1]
    scale = jnp.float32(rows * groups * n) / total[0:1, 0:1]
    position = lax.broadcasted_iota(jnp.int32, (rows, 1), 0)
    factor = jnp.where(position < count, 1.0, 0.0) * scale

    lane = lax.broadcasted_iota(jnp.int32, (rows, 128), 1)
    columns_ref[...] = jnp.where(
        lane == 0, gate * factor, 0.0
    )

    own_act.wait()
    near_act.wait()
    for part in range(pieces):
        for j in range(2, n):
            remote(ACT, act_out, act_home, j, part, far_at(part, j), ROWS).wait()
    act = jnp.dot(unplace[...], act_home[...], preferred_element_type=jnp.float32)
    mixed_ref[...] = (gate * act).astype(jnp.bfloat16)
    dots = jnp.sum(act * cot[...].astype(jnp.float32), axis=1, keepdims=True) * factor
    gate_grad_ref[...] = jnp.transpose(jnp.broadcast_to(dots, (rows, 128)))[0:1, :]

    own_grad.wait()
    near_grad.wait()
    for part in range(pieces):
        for j in range(2, n):
            remote(GRAD, grad_out, grad_home, j, part, far_at(part, j), ROWS).wait()


def finish(
    mixed, gate_grad, grad_home, unplace, columns,
    mixed_hbm, grad_hbm, gate_grad_ref, grad_v, store_sem,
):
    depth = grad_v.shape[1]
    store_mixed = pltpu.make_async_copy(mixed, mixed_hbm, store_sem.at[0])
    store_mixed.start()
    both = columns[:, 0:1]
    width = tile_of(depth, 512)
    stores = []
    for i in range(depth // width):
        cut = pl.ds(i * width, width)
        grad_v[:, cut] = (
            jnp.dot(unplace[...], grad_home[:, cut], preferred_element_type=jnp.float32) * both
        ).astype(jnp.bfloat16)
        store = pltpu.make_async_copy(grad_v.at[:, cut], grad_hbm.at[:, cut], store_sem.at[1 + i])
        store.start()
        stores.append(store)
    gate_grad_ref[...] = gate_grad[...]
    store_mixed.wait()
    for store in stores:
        store.wait()


def pinned(array):
    return pltpu.with_memory_space_constraint(array, pltpu.HBM)


def solution(mesh):
    n = mesh.shape["expert"]
    groups = mesh.shape["dp"]

    def shards(tokens, routes, gates, counts, expert_weight, cotangent):
        rows, depth = tokens.shape
        units = cotangent.shape[1]
        cap = -(-(3 * rows // (2 * n)) // ROWS) * ROWS
        slots = n * cap
        pieces = cap // ROWS
        small = max(2 * cap, (n - 2) * ROWS)
        bf16 = jnp.bfloat16
        hbm = pl.BlockSpec(memory_space=pltpu.HBM)
        free = pl.BlockSpec(memory_space=pl.ANY)
        vmem = pl.BlockSpec(memory_space=pltpu.VMEM)
        mixed, gate_grad, grad_home, unplace, columns = pl.pallas_call(
            functools.partial(kernel, n, groups, cap),
            out_shape=(
                jax.ShapeDtypeStruct((rows, units), bf16),
                jax.ShapeDtypeStruct((1, rows), jnp.float32),
                jax.ShapeDtypeStruct((slots, depth), bf16),
                jax.ShapeDtypeStruct((rows, slots), bf16),
                jax.ShapeDtypeStruct((rows, 128), jnp.float32),
            ),
            in_specs=[hbm, hbm, pl.BlockSpec(memory_space=pltpu.SMEM), hbm, hbm, hbm],
            out_specs=(vmem, vmem, free, vmem, vmem),
            scratch_shapes=[
                pltpu.VMEM((1, rows), jnp.int32),
                pltpu.VMEM((1, rows), jnp.float32),
                pltpu.VMEM((rows, depth), bf16),
                pltpu.VMEM((rows, units), bf16),
                pltpu.VMEM((depth, units), bf16),
                pltpu.VMEM((slots, rows), bf16),
                pltpu.VMEM((slots, depth), bf16),
                pltpu.VMEM((slots, units), bf16),
                pltpu.VMEM((slots, depth), bf16),
                pltpu.VMEM((slots, units), bf16),
                pltpu.VMEM((small, units), bf16),
                pltpu.VMEM((slots, units), bf16),
                pltpu.VMEM((slots, units), bf16),
                pltpu.VMEM((slots, depth), bf16),
                pltpu.VMEM((8, 128), jnp.float32),
                pltpu.VMEM((groups - 1, 8, 128), jnp.float32),
                pltpu.VMEM((8, 128), jnp.float32),
                pltpu.VMEM((n - 1, 8, 128), jnp.float32),
                pltpu.SemaphoreType.DMA((5,)),
                pltpu.SemaphoreType.DMA((4, n, pieces)),
                pltpu.SemaphoreType.DMA((4, n, pieces)),
                pltpu.SemaphoreType.DMA((groups - 1 + n - 1,)),
                pltpu.SemaphoreType.DMA((groups - 1 + n - 1,)),
            ],
            compiler_params=pltpu.CompilerParams(
                collective_id=0, has_side_effects=True, vmem_limit_bytes=40 * 1024 * 1024
            ),
        )(
            pinned(routes.reshape(1, rows)),
            pinned(gates.reshape(1, rows)),
            counts,
            pinned(tokens),
            pinned(expert_weight),
            pinned(cotangent),
        )
        mixed, token_grad, gate_grad = pl.pallas_call(
            finish,
            out_shape=(
                jax.ShapeDtypeStruct((rows, units), bf16),
                jax.ShapeDtypeStruct((rows, depth), bf16),
                jax.ShapeDtypeStruct((1, rows), jnp.float32),
            ),
            in_specs=[vmem, vmem, vmem, vmem, vmem],
            out_specs=(hbm, hbm, vmem),
            scratch_shapes=[
                pltpu.VMEM((rows, depth), bf16),
                pltpu.SemaphoreType.DMA((1 + depth // tile_of(depth, 512),)),
            ],
            compiler_params=pltpu.CompilerParams(vmem_limit_bytes=24 * 1024 * 1024),
        )(mixed, gate_grad, grad_home, unplace, columns)
        return (mixed, token_grad, gate_grad.reshape(rows, 1))

    spread = P(("dp", "expert"), None)
    return jax.shard_map(
        shards,
        mesh=mesh,
        in_specs=(spread, spread, spread, P(("dp", "expert")), P("expert", None, None), spread),
        out_specs=(spread, spread, spread),
        check_vma=False,
    )
```

```python
import functools

import jax
import jax.numpy as jnp
from jax import lax
from jax.experimental import pallas as pl
from jax.experimental.pallas import tpu as pltpu
from jax.sharding import PartitionSpec as P

MESH = pl.DeviceIdType.MESH
ROWS = 16
TOK, COT, ACT, GRAD = 0, 1, 2, 3


def tile_of(size, most):
    tile = most
    while size % tile:
        tile //= 2
    return tile


def kernel(
    n, groups, cap, routes_hbm, gates_hbm, counts_ref, tokens_hbm, weight_hbm, cotangent_hbm,
    mixed_ref, gate_grad_ref, grad_home, unplace, columns_ref,
    routes_ref, gates_ref, tok, cot, w, place, tok_out, cot_out, tok_in, cot_in, delta,
    act_out, act_home, grad_out, cnt_mine, cnt_dp, cnt_sum, cnt_ex,
    load_sem, send_sem, recv_sem, cnt_send, cnt_recv,
):
    rows, depth = tok.shape
    units = cot.shape[1]
    slots = n * cap
    pieces = cap // ROWS
    far = n - 2
    step = far * ROWS
    me = lax.axis_index("expert")
    group = lax.axis_index("dp")

    barrier = pltpu.get_barrier_semaphore()
    for j in range(1, n):
        pl.semaphore_signal(
            barrier, inc=1, device_id=(group, lax.bitwise_xor(me, j)), device_id_type=MESH
        )
    for k in range(1, groups):
        pl.semaphore_signal(
            barrier, inc=1, device_id=(lax.rem(group + k, groups), me), device_id_type=MESH
        )

    load_tok = pltpu.make_async_copy(tokens_hbm, tok, load_sem.at[0])
    load_cot = pltpu.make_async_copy(cotangent_hbm, cot, load_sem.at[1])
    load_w = pltpu.make_async_copy(weight_hbm.at[0], w, load_sem.at[2])
    load_routes = pltpu.make_async_copy(routes_hbm, routes_ref, load_sem.at[3])
    load_gates = pltpu.make_async_copy(gates_hbm, gates_ref, load_sem.at[4])
    load_routes.start()
    load_gates.start()
    load_tok.start()
    load_cot.start()

    load_routes.wait()
    load_gates.wait()
    route = routes_ref[...]
    high = -(-n // ROWS) * ROWS
    choose = lax.broadcasted_iota(jnp.int32, (high, rows), 0) == route
    choose_f = jnp.where(choose, 1.0, 0.0)
    upper = jnp.where(
        lax.broadcasted_iota(jnp.int32, (rows, rows), 0)
        <= lax.broadcasted_iota(jnp.int32, (rows, rows), 1),
        1.0,
        0.0,
    ).astype(jnp.bfloat16)
    running = jnp.dot(choose_f.astype(jnp.bfloat16), upper, preferred_element_type=jnp.float32)
    rank = (jnp.sum(running * choose_f, axis=0, keepdims=True) - 1.0).astype(jnp.int32)
    rel = lax.bitwise_xor(route, jnp.full(route.shape, me, jnp.int32))
    piece = lax.div(rank, jnp.int32(ROWS))
    slot = jnp.where(
        rel < 2,
        rel * cap + rank,
        2 * cap + piece * step + (rel - 2) * ROWS + (rank - piece * ROWS),
    )
    place[...] = jnp.where(
        lax.broadcasted_iota(jnp.int32, (slots, rows), 0) == slot, 1.0, 0.0
    ).astype(jnp.bfloat16)
    line = lax.broadcasted_iota(jnp.int32, (128, rows), 0)
    columns = jnp.transpose(
        jnp.where(line == 0, gates_ref[...], jnp.where(line == 1, slot.astype(jnp.float32), 0.0))
    )
    gate = columns[:, 0:1]
    unplace[...] = jnp.where(
        lax.broadcasted_iota(jnp.int32, (rows, slots), 1) == columns[:, 1:2].astype(jnp.int32),
        1.0,
        0.0,
    ).astype(jnp.bfloat16)
    count = counts_ref[0]
    cnt_mine[...] = jnp.full(cnt_mine.shape, count.astype(jnp.float32), jnp.float32)

    def remote(kind, source, target, j, part, at, size):
        return pltpu.make_async_remote_copy(
            src_ref=source.at[pl.ds(at, size)],
            dst_ref=target.at[pl.ds(at, size)],
            send_sem=send_sem.at[kind, j, part],
            recv_sem=recv_sem.at[kind, j, part],
            device_id=(group, lax.bitwise_xor(me, j)),
            device_id_type=MESH,
        )

    def gather(source, target, at, size):
        width = tile_of(source.shape[1], 512)

        def body(i, carry):
            cut = pl.ds(pl.multiple_of(i * width, width), width)
            target[at : at + size, cut] = jnp.dot(
                place[at : at + size, :], source[:, cut], preferred_element_type=jnp.float32
            ).astype(jnp.bfloat16)
            return carry

        lax.fori_loop(0, source.shape[1] // width, body, 0)

    def far_at(part, j):
        return 2 * cap + part * step + (j - 2) * ROWS

    out = []

    def send_far(part):
        gather(tok, tok_out, 2 * cap + part * step, step)
        if part == 0:
            pl.semaphore_wait(barrier, n - 1 + groups - 1)
        for j in range(2, n):
            copy = remote(TOK, tok_out, tok_in, j, part, far_at(part, j), ROWS)
            copy.start()
            out.append(copy)
        if part == 0:
            load_cot.wait()
            load_w.start()
        gather(cot, cot_out, 2 * cap + part * step, step)
        for j in range(2, n):
            copy = remote(COT, cot_out, cot_in, j, part, far_at(part, j), ROWS)
            copy.start()
            out.append(copy)

    early = pieces
    load_tok.wait()
    send_far(0)
    gather(tok, tok_out, cap, cap)
    near_tok = remote(TOK, tok_out, tok_in, 1, 0, cap, cap)
    near_tok.start()
    gather(cot, cot_out, cap, cap)
    near_cot = remote(COT, cot_out, cot_in, 1, 0, cap, cap)
    near_cot.start()
    for part in range(1, early):
        send_far(part)

    counts = []
    for k in range(1, groups):
        copy = pltpu.make_async_remote_copy(
            src_ref=cnt_mine,
            dst_ref=cnt_dp.at[k - 1],
            send_sem=cnt_send.at[k - 1],
            recv_sem=cnt_recv.at[k - 1],
            device_id=(lax.rem(group + k, groups), me),
            device_id_type=MESH,
        )
        copy.start()
        counts.append(copy)

    gather(tok, tok_in, 0, cap)
    gather(cot, cot_in, 0, cap)

    def forward(at, size):
        width = tile_of(units, 256)

        def body(i, carry):
            cut = pl.ds(pl.multiple_of(i * width, width), width)
            pre = jnp.dot(
                tok_in[at : at + size, :], w[:, cut], preferred_element_type=jnp.float32
            )
            sig = jax.nn.sigmoid(pre)
            act = (pre * sig).astype(jnp.bfloat16)
            act_out[at : at + size, cut] = act
            slope = sig * (1.0 + pre * (1.0 - sig))
            delta[0:size, cut] = (
                cot_in[at : at + size, cut].astype(jnp.float32) * slope
            ).astype(jnp.bfloat16)
            return carry

        lax.fori_loop(0, units // width, body, 0)

    def backward(at, size):
        width = tile_of(depth, 512)

        def body(i, carry):
            cut = pl.ds(pl.multiple_of(i * width, width), width)
            grad = lax.dot_general(
                delta[0:size, :], w[cut, :], (((1,), (1,)), ((), ())),
                preferred_element_type=jnp.float32,
            ).astype(jnp.bfloat16)
            grad_out[at : at + size, cut] = grad
            return carry

        lax.fori_loop(0, depth // width, body, 0)

    load_w.wait()
    near_tok.wait_recv()
    near_cot.wait_recv()
    forward(0, 2 * cap)
    near_act = remote(ACT, act_out, act_home, 1, 0, cap, cap)
    near_act.start()
    own_act = pltpu.make_async_copy(
        act_out.at[pl.ds(0, cap)], act_home.at[pl.ds(0, cap)], load_sem.at[0]
    )
    own_act.start()
    backward(0, 2 * cap)
    near_grad = remote(GRAD, grad_out, grad_home, 1, 0, cap, cap)
    near_grad.start()
    own_grad = pltpu.make_async_copy(
        grad_out.at[pl.ds(0, cap)], grad_home.at[pl.ds(0, cap)], load_sem.at[1]
    )
    own_grad.start()
    for part in range(early, pieces):
        send_far(part)

    for copy in counts:
        copy.wait_recv()
    partial = cnt_mine[...]
    for k in range(1, groups):
        partial = partial + cnt_dp[k - 1]
    cnt_sum[...] = partial
    sums = []
    for j in range(1, n):
        copy = pltpu.make_async_remote_copy(
            src_ref=cnt_sum,
            dst_ref=cnt_ex.at[j - 1],
            send_sem=cnt_send.at[groups - 1 + j - 1],
            recv_sem=cnt_recv.at[groups - 1 + j - 1],
            device_id=(group, lax.bitwise_xor(me, j)),
            device_id_type=MESH,
        )
        copy.start()
        sums.append(copy)

    for part in range(pieces):
        at = 2 * cap + part * step
        for kind in (TOK, COT):
            for j in range(2, n):
                if kind == TOK:
                    remote(TOK, tok_out, tok_in, j, part, far_at(part, j), ROWS).wait_recv()
                else:
                    remote(COT, cot_out, cot_in, j, part, far_at(part, j), ROWS).wait_recv()
        forward(at, step)
        for j in range(2, n):
            copy = remote(ACT, act_out, act_home, j, part, far_at(part, j), ROWS)
            copy.start()
        backward(at, step)
        for j in range(2, n):
            copy = remote(GRAD, grad_out, grad_home, j, part, far_at(part, j), ROWS)
            copy.start()

    for copy in out:
        copy.wait_send()
    near_tok.wait_send()
    near_cot.wait_send()
    for copy in counts:
        copy.wait_send()
    for copy in sums:
        copy.wait()
    total = partial
    for j in range(1, n):
        total = total + cnt_ex[j - 1]
    scale = jnp.float32(rows * groups * n) / total[0:1, 0:1]
    position = lax.broadcasted_iota(jnp.int32, (rows, 1), 0)
    factor = jnp.where(position < count, 1.0, 0.0) * scale

    lane = lax.broadcasted_iota(jnp.int32, (rows, 128), 1)
    columns_ref[...] = jnp.where(
        lane == 0, gate * factor, 0.0
    )

    own_act.wait()
    near_act.wait()
    for part in range(pieces):
        for j in range(2, n):
            remote(ACT, act_out, act_home, j, part, far_at(part, j), ROWS).wait()
    act = jnp.dot(unplace[...], act_home[...], preferred_element_type=jnp.float32)
    mixed_ref[...] = (gate * act).astype(jnp.bfloat16)
    dots = jnp.sum(act * cot[...].astype(jnp.float32), axis=1, keepdims=True) * factor
    gate_grad_ref[...] = jnp.transpose(jnp.broadcast_to(dots, (rows, 128)))[0:1, :]

    own_grad.wait()
    near_grad.wait()
    for part in range(pieces):
        for j in range(2, n):
            remote(GRAD, grad_out, grad_home, j, part, far_at(part, j), ROWS).wait()


def finish(
    mixed, gate_grad, grad_home, unplace, columns,
    mixed_hbm, grad_hbm, gate_grad_ref, grad_v, store_sem,
):
    depth = grad_v.shape[1]
    store_mixed = pltpu.make_async_copy(mixed, mixed_hbm, store_sem.at[0])
    store_mixed.start()
    both = columns[:, 0:1]
    width = tile_of(depth, 512)
    stores = []
    for i in range(depth // width):
        cut = pl.ds(i * width, width)
        grad_v[:, cut] = (
            jnp.dot(unplace[...], grad_home[:, cut], preferred_element_type=jnp.float32) * both
        ).astype(jnp.bfloat16)
        store = pltpu.make_async_copy(grad_v.at[:, cut], grad_hbm.at[:, cut], store_sem.at[1 + i])
        store.start()
        stores.append(store)
    gate_grad_ref[...] = gate_grad[...]
    store_mixed.wait()
    for store in stores:
        store.wait()


def pinned(array):
    return pltpu.with_memory_space_constraint(array, pltpu.HBM)


def solution(mesh):
    n = mesh.shape["expert"]
    groups = mesh.shape["dp"]

    def shards(tokens, routes, gates, counts, expert_weight, cotangent):
        rows, depth = tokens.shape
        units = cotangent.shape[1]
        cap = -(-(3 * rows // (2 * n)) // ROWS) * ROWS
        slots = n * cap
        pieces = cap // ROWS
        small = max(2 * cap, (n - 2) * ROWS)
        bf16 = jnp.bfloat16
        hbm = pl.BlockSpec(memory_space=pltpu.HBM)
        free = pl.BlockSpec(memory_space=pl.ANY)
        vmem = pl.BlockSpec(memory_space=pltpu.VMEM)
        mixed, gate_grad, grad_home, unplace, columns = pl.pallas_call(
            functools.partial(kernel, n, groups, cap),
            out_shape=(
                jax.ShapeDtypeStruct((rows, units), bf16),
                jax.ShapeDtypeStruct((1, rows), jnp.float32),
                jax.ShapeDtypeStruct((slots, depth), bf16),
                jax.ShapeDtypeStruct((rows, slots), bf16),
                jax.ShapeDtypeStruct((rows, 128), jnp.float32),
            ),
            in_specs=[hbm, hbm, pl.BlockSpec(memory_space=pltpu.SMEM), hbm, hbm, hbm],
            out_specs=(vmem, vmem, free, vmem, vmem),
            scratch_shapes=[
                pltpu.VMEM((1, rows), jnp.int32),
                pltpu.VMEM((1, rows), jnp.float32),
                pltpu.VMEM((rows, depth), bf16),
                pltpu.VMEM((rows, units), bf16),
                pltpu.VMEM((depth, units), bf16),
                pltpu.VMEM((slots, rows), bf16),
                pltpu.VMEM((slots, depth), bf16),
                pltpu.VMEM((slots, units), bf16),
                pltpu.VMEM((slots, depth), bf16),
                pltpu.VMEM((slots, units), bf16),
                pltpu.VMEM((small, units), bf16),
                pltpu.VMEM((slots, units), bf16),
                pltpu.VMEM((slots, units), bf16),
                pltpu.VMEM((slots, depth), bf16),
                pltpu.VMEM((8, 128), jnp.float32),
                pltpu.VMEM((groups - 1, 8, 128), jnp.float32),
                pltpu.VMEM((8, 128), jnp.float32),
                pltpu.VMEM((n - 1, 8, 128), jnp.float32),
                pltpu.SemaphoreType.DMA((5,)),
                pltpu.SemaphoreType.DMA((4, n, pieces)),
                pltpu.SemaphoreType.DMA((4, n, pieces)),
                pltpu.SemaphoreType.DMA((groups - 1 + n - 1,)),
                pltpu.SemaphoreType.DMA((groups - 1 + n - 1,)),
            ],
            compiler_params=pltpu.CompilerParams(
                collective_id=0, has_side_effects=True, vmem_limit_bytes=40 * 1024 * 1024
            ),
        )(
            pinned(routes.reshape(1, rows)),
            pinned(gates.reshape(1, rows)),
            counts,
            pinned(tokens),
            pinned(expert_weight),
            pinned(cotangent),
        )
        mixed, token_grad, gate_grad = pl.pallas_call(
            finish,
            out_shape=(
                jax.ShapeDtypeStruct((rows, units), bf16),
                jax.ShapeDtypeStruct((rows, depth), bf16),
                jax.ShapeDtypeStruct((1, rows), jnp.float32),
            ),
            in_specs=[vmem, vmem, vmem, vmem, vmem],
            out_specs=(hbm, hbm, vmem),
            scratch_shapes=[
                pltpu.VMEM((rows, depth), bf16),
                pltpu.SemaphoreType.DMA((1 + depth // tile_of(depth, 512),)),
            ],
            compiler_params=pltpu.CompilerParams(vmem_limit_bytes=24 * 1024 * 1024),
        )(mixed, gate_grad, grad_home, unplace, columns)
        return (mixed, token_grad, gate_grad.reshape(rows, 1))

    spread = P(("dp", "expert"), None)
    return jax.shard_map(
        shards,
        mesh=mesh,
        in_specs=(spread, spread, spread, P(("dp", "expert")), P("expert", None, None), spread),
        out_specs=(spread, spread, spread),
        check_vma=False,
    )
```
